128 devices in a mesh: chan: 64 (over y, x, z_hi, core), win: 2 (over z_lo).
Axes of the slice: x: 4, y: 4, z: 4 (z_hi: 2, z_lo: 2; z = z_hi * 2 + z_lo), core: 2. Of those that a mesh axis runs over, the one named last changes fastest.
Arguments:
- signal: bfloat16 [2048, 256, 1024], P('chan', 'win'), may hold values from -6 to 6
- valid: int32 [2048, 256], P('chan', 'win'), may hold values 0 or 1
- owners: int32 [3], replicated, may hold values from 0 to 63
Outputs:
- cross: bfloat16 [2, 3, 192, 2048, 32], P(None, None, 'win', 'chan')
The draws below stay inside these ranges and needn't reach their ends.
Inputs may be any that keep to these rules, and one draw needn't show every extreme that they name: owners[s] names an index of chan; steps may repeat a block.
All inputs are finite; a program needn't handle non-finite values. No bound on the sum of `valid` on one device may be relied on, other than what follows from the above.
Results may differ from the reference program's by a relative error of at most 0.0066.
Values may be sent and summed in bfloat16 or wider, within the bound.
No kernel may reach another device: no remote copies, remote signals or barrier semaphores. Data moves between devices by JAX's collectives and lax.ppermute only.
A program may use at most 128 MiB of HBM per device.

```python
import math
import jax
import jax.numpy as jnp
from jax import lax

SAMPLES = 1024
BINS = 192
FIRST_BIN = 32
WINDOWS = 256
CH_DEV = 32
STEPS = 3
CHANNELS = 2048
N_CHAN = 64


def with_ends(drawn, stream_key, low, largest):
    longest = drawn.shape.index(max(drawn.shape))
    spots = []
    for shift in (0, 1):
        where = [jax.random.randint(jax.random.fold_in(stream_key, axis), (), 0, length) for axis, length in enumerate(drawn.shape)]
        where[longest] = (where[longest] + shift) % drawn.shape[longest]
        spots.append(tuple(where))
    return drawn.at[spots[0]].set(low).at[spots[1]].set(largest)


def shard_levels(own_key, shape, split, smallest, high):
    factor_of, own = 1.0, jax.random.fold_in(own_key, 6)
    for axis_at, parts in split:
        heights = jnp.exp(jax.random.uniform(jax.random.fold_in(own, axis_at), (parts,), jnp.float32, smallest / len(split), high / len(split)))
        factor_of = factor_of * jnp.repeat(heights, shape[axis_at] // parts).reshape([-1 if axis == axis_at else 1 for axis in range(len(shape))])
    return factor_of


def scatter_about(stream_key, dims, spread, bound, split=(), kind=jnp.bfloat16):
    gain = shard_levels(stream_key, dims, split, -0.22, 0.18) if split else 1.0
    values = jax.random.normal(stream_key, dims, jnp.float32) * spread * gain
    return jnp.minimum(jnp.maximum(values, -bound), bound).astype(kind)


def setup_inputs(seed: int = 0) -> dict:
    keys = jax.random.split(jax.random.key(seed), 4)
    return {
        "signal": scatter_about(keys[0], (CHANNELS, WINDOWS, SAMPLES), 1.0, 6.0, ((0, 64), (1, 2))),
        "valid": with_ends((jax.random.randint(keys[1], (CHANNELS, WINDOWS), 0, 4) < 3).astype(jnp.int32), jax.random.fold_in(keys[1], 1), 0, 1),
        "owners": jax.random.randint(keys[2], (STEPS,), 0, N_CHAN).astype(jnp.int32),
    }


def band_table(samples, bins, first):
    times = jnp.arange(samples, dtype=jnp.int32)
    freqs = first + jnp.arange(bins, dtype=jnp.int32)
    phase = (freqs[:, None] * times[None, :] % samples).astype(jnp.float32) * (2.0 * math.pi / samples)
    taper = 0.5 - 0.5 * jnp.cos(times.astype(jnp.float32) * (2.0 * math.pi / samples))
    rows = jnp.concatenate([jnp.cos(phase) * taper[None, :], -jnp.sin(phase) * taper[None, :]], axis=0)
    return rows.astype(jnp.bfloat16)

def whiten(table, samples_block, valid_block):
    count, windows, samples = samples_block.shape
    flat = samples_block.reshape(count * windows, samples)
    spec = lax.dot_general(table, flat, (((1,), (1,)), ((), ())), preferred_element_type=jnp.float32)
    spec = spec.reshape(2, table.shape[0] // 2, count, windows)
    power = lax.optimization_barrier(jnp.mean(spec[0] * spec[0] + spec[1] * spec[1], axis=0))
    factor = lax.rsqrt(power + 1e-06) * valid_block.astype(jnp.float32)
    return (spec * factor[None, None]).astype(jnp.bfloat16)

def reference(signal, valid, owners):
    table = band_table(SAMPLES, BINS, FIRST_BIN)
    groups = CHANNELS // CH_DEV
    sig_blocks = signal.reshape(groups, CH_DEV, WINDOWS, SAMPLES)
    mask_blocks = valid.reshape(groups, CH_DEV, WINDOWS)
    spectra = lax.map(lambda pair: whiten(table, pair[0], pair[1]), (sig_blocks, mask_blocks))
    by_bin = jnp.transpose(spectra, (2, 1, 0, 3, 4)).reshape(BINS, 2, CHANNELS, WINDOWS)
    factor = 1.0 / math.sqrt(WINDOWS)

    def product(left, right):
        return jnp.dot(left, right.T, preferred_element_type=jnp.float32)

    def one_step(owner):
        start = (owner * CH_DEV).astype(jnp.int32)
        block = lax.dynamic_slice_in_dim(by_bin, start, CH_DEV, 2)

        def one_bin(pair):
            mine, theirs = pair
            real = product(mine[0], theirs[0]) + product(mine[1], theirs[1])
            imag = product(mine[1], theirs[0]) - product(mine[0], theirs[1])
            return jnp.stack([real, imag]) * factor
        return lax.map(one_bin, (by_bin, block))
    result = lax.map(one_step, owners)
    return jnp.transpose(result, (2, 0, 1, 3, 4)).astype(jnp.bfloat16)
```

```python
import math

import jax
import jax.numpy as jnp
from jax import lax
from jax.sharding import PartitionSpec as P

SAMPLES = 1024
BINS = 192
FIRST_BIN = 32
WINDOWS = 256
STEPS = 3
CH_DEV = 32
N_CHAN = 64


def band_table(samples, bins, first):
    times = jnp.arange(samples, dtype=jnp.int32)
    freqs = first + jnp.arange(bins, dtype=jnp.int32)
    phase = (freqs[:, None] * times[None, :] % samples).astype(jnp.float32) * (
        2.0 * math.pi / samples
    )
    taper = 0.5 - 0.5 * jnp.cos(times.astype(jnp.float32) * (2.0 * math.pi / samples))
    rows = jnp.concatenate(
        [jnp.cos(phase) * taper[None, :], -jnp.sin(phase) * taper[None, :]], axis=0
    )
    return rows.astype(jnp.bfloat16)


def whiten(table, samples_block, valid_block):
    count, windows, samples = samples_block.shape
    flat = samples_block.reshape(count * windows, samples)
    spec = lax.dot_general(
        table, flat, (((1,), (1,)), ((), ())), preferred_element_type=jnp.float32
    )
    spec = spec.reshape(2, table.shape[0] // 2, count, windows)
    power = jnp.mean(spec[0] * spec[0] + spec[1] * spec[1], axis=0)
    factor = lax.rsqrt(power + 1e-06) * valid_block.astype(jnp.float32)
    return (spec * factor[None, None]).astype(jnp.bfloat16)


def by_destination(white):
    parts = white.reshape(2, 2, 3, 32, CH_DEV, 128)
    full = jnp.stack([parts[:, :, 0], parts[:, :, 2]], axis=0)
    full = jnp.transpose(full, (3, 0, 2, 1, 4, 5))
    mid = parts[:, :, 1].reshape(2, 2, 32, 2, 16, 128)
    mid = jnp.transpose(mid, (2, 3, 1, 0, 4, 5))
    return jnp.concatenate([full, mid], axis=4).reshape(128, 2, 48, 128)


def against(left, block):
    swapped = jnp.stack([-block[:, :, 1], block[:, :, 0]], axis=2)
    both = jnp.stack([block, swapped])
    return jnp.einsum("iwrct,qswrjt->icqsj", left, both, preferred_element_type=jnp.float32)


def per_device(signal, valid, owners):
    table = band_table(SAMPLES, BINS, FIRST_BIN)
    white = whiten(table, signal, valid)
    got = lax.all_to_all(by_destination(white), ("chan", "win"), 0, 0, tiled=True)
    got = got.reshape(N_CHAN, 2, 2, 48, 128)
    planned = jnp.stack([lax.dynamic_index_in_dim(got, owners[s], 0, False) for s in range(STEPS)])
    own = planned[:, :, :, 32:]
    other = lax.ppermute(own, "chan", [(i, i ^ 1) for i in range(N_CHAN)])
    first = (lax.axis_index("chan") & 1) == 0
    mid_block = jnp.where(
        first, jnp.concatenate([own, other], axis=3), jnp.concatenate([other, own], axis=3)
    )
    full = against(got[:, :, :, :32], planned[:, :, :, :32])
    mid = against(got[:, :, :, 32:], mid_block)
    result = jnp.concatenate([full, mid], axis=1) * (1.0 / math.sqrt(WINDOWS))
    result = result.astype(jnp.bfloat16).reshape(N_CHAN, 72, 128)
    back = lax.all_to_all(result, "chan", 0, 0, tiled=True)
    back = back.reshape(32, 2, 48, 2, STEPS, 32)
    low, high = back[:, 0, :32], back[:, 1, :32]
    middle = jnp.concatenate([back[:, 0, 32:], back[:, 1, 32:]], axis=1)
    out = jnp.stack([low, middle, high])
    return jnp.transpose(out, (3, 4, 0, 1, 2, 5)).reshape(2, STEPS, 96, 32, 32)


def solution(mesh):
    in_specs = (P("chan", "win", None), P("chan", "win"), P())
    out_specs = P(None, None, "win", "chan", None)
    return jax.shard_map(
        per_device, mesh=mesh, in_specs=in_specs, out_specs=out_specs, check_vma=False
    )
```

```python
import math

import jax
import jax.numpy as jnp
from jax import lax
from jax.experimental import pallas as pl
from jax.experimental.pallas import tpu as pltpu
from jax.sharding import PartitionSpec as P

SAMPLES = 1024
BINS = 192
WINDOWS = 256
STEPS = 3
CH_DEV = 32
N_CHAN = 64
LANES = 128
COLUMNS = 2 * STEPS * CH_DEV
FULL_ROWS, ROWS = 48, 72


def vmem():
    return pl.BlockSpec(memory_space=pltpu.VMEM)


def limit(mib):
    return pltpu.CompilerParams(vmem_limit_bytes=mib << 20)


def angles(rows, scale):
    times = lax.broadcasted_iota(jnp.int32, (rows, SAMPLES), 1)
    freqs = lax.broadcasted_iota(jnp.int32, (rows, SAMPLES), 0) * scale
    return (freqs * times % SAMPLES).astype(jnp.float32) * (2.0 * math.pi / SAMPLES)


def fill_table(table):
    fine = angles(32, 1)
    coarse = angles(8, 32)
    times = lax.broadcasted_iota(jnp.int32, (1, SAMPLES), 1).astype(jnp.float32)
    taper = 0.5 - 0.5 * jnp.cos(times * (2.0 * math.pi / SAMPLES))
    fine_cos, fine_sin = jnp.cos(fine) * taper, jnp.sin(fine) * taper
    coarse_cos, coarse_sin = jnp.cos(coarse), jnp.sin(coarse)
    for a in range(6):
        cos_a, sin_a = coarse_cos[a + 1 : a + 2], coarse_sin[a + 1 : a + 2]
        real = cos_a * fine_cos - sin_a * fine_sin
        imag = -sin_a * fine_cos - cos_a * fine_sin
        table[32 * a : 32 * a + 32, :] = real.astype(jnp.bfloat16)
        table[BINS + 32 * a : BINS + 32 * a + 32, :] = imag.astype(jnp.bfloat16)


def whiten_kernel(signal, valid, out, table, white):
    g = pl.program_id(0)

    @pl.when(g == 0)
    def _():
        fill_table(table)

    weights = valid[...].astype(jnp.float32)
    for pair in range(8):
        both = signal[2 * pair : 2 * pair + 2].reshape(2 * LANES, SAMPLES)
        spec = lax.dot_general(
            table[...], both, (((1,), (1,)), ((), ())), preferred_element_type=jnp.float32
        )
        power = jnp.sum(spec * spec, axis=0, keepdims=True) * (1.0 / BINS)
        factor = lax.rsqrt(power + 1e-06)
        for one in range(2):
            c = 2 * pair + one
            lanes = slice(one * LANES, (one + 1) * LANES)
            scale = factor[:, lanes] * weights[c : c + 1, :]
            white[c] = (spec[:, lanes] * scale).astype(jnp.bfloat16)
    own_rows = pl.ds(pl.multiple_of(16 * g, 16), 16)
    for h in range(2):
        for r in range(2):
            for m in range(3):
                start = BINS * r + 96 * h + 32 * m
                rows = jnp.swapaxes(white[:, start : start + 32, :], 0, 1)
                if m == 2:
                    out[:, g, h, r, 32:48, :] = rows
                else:
                    out[16 * m : 16 * m + 16, :, h, r, own_rows, :] = rows.reshape(16, 2, 16, LANES)


def whitened(signal, valid):
    return pl.pallas_call(
        whiten_kernel,
        grid=(2,),
        in_specs=[
            pl.BlockSpec((16, LANES, SAMPLES), lambda g: (g, 0, 0)),
            pl.BlockSpec((16, LANES), lambda g: (g, 0)),
        ],
        out_specs=vmem(),
        out_shape=jax.ShapeDtypeStruct((32, 2, 2, 2, 48, LANES), jnp.bfloat16),
        scratch_shapes=[
            pltpu.VMEM((2 * BINS, SAMPLES), jnp.bfloat16),
            pltpu.VMEM((16, 2 * BINS, LANES), jnp.bfloat16),
        ],
        compiler_params=limit(54),
        cost_estimate=pl.CostEstimate(
            flops=2 * 2 * BINS * SAMPLES * 4096, bytes_accessed=12 << 20, transcendentals=0
        ),
        name="whiten",
    )(signal, valid)


def pick_kernel(owners, got, out):
    for s in range(STEPS):
        out[s] = got[owners[s], :, :, 32:48, :]


def picked(owners, got):
    return pl.pallas_call(
        pick_kernel,
        in_specs=[pl.BlockSpec(memory_space=pltpu.SMEM), vmem()],
        out_specs=vmem(),
        out_shape=jax.ShapeDtypeStruct((STEPS, 2, 2, 16, LANES), jnp.bfloat16),
        compiler_params=limit(16),
        cost_estimate=pl.CostEstimate(flops=0, bytes_accessed=98304, transcendentals=0),
        name="pick",
    )(owners, got)


def planned_columns(planned):
    real = [jnp.concatenate([b[0, 0], b[0, 1], b[1, 0], b[1, 1]], axis=1) for b in planned]
    imag = [jnp.concatenate([-b[0, 1], b[0, 0], -b[1, 1], b[1, 0]], axis=1) for b in planned]
    return jnp.concatenate(real + imag, axis=0)


def products(left, columns):
    count, channels = left.shape[0], left.shape[3]
    rows = jnp.concatenate(
        [left[:, w, r].reshape(count * channels, LANES) for w in range(2) for r in range(2)], axis=1
    )
    result = lax.dot_general(
        rows, columns, (((1,), (1,)), ((), ())), preferred_element_type=jnp.float32
    )
    return (result * (1.0 / math.sqrt(WINDOWS))).reshape(count, channels, COLUMNS)


def packed(result):
    rest = result[:, :, LANES:]
    parts = [result[:, :, :LANES]]
    for start in range(0, result.shape[1], 16):
        parts.append(
            jnp.concatenate([rest[:, start : start + 8], rest[:, start + 8 : start + 16]], axis=2)
        )
    return jnp.concatenate(parts, axis=1).astype(jnp.bfloat16)


def full_kernel(owners, got, out, columns):
    columns[...] = planned_columns([got[owners[s], :, :, :32, :] for s in range(STEPS)])
    for start in range(0, N_CHAN, 8):
        left = got[start : start + 8, :, :, :32, :]
        out[start : start + 8, :FULL_ROWS, :] = packed(products(left, columns[...]))


def cross_full(owners, got):
    return pl.pallas_call(
        full_kernel,
        in_specs=[pl.BlockSpec(memory_space=pltpu.SMEM), vmem()],
        out_specs=vmem(),
        out_shape=jax.ShapeDtypeStruct((N_CHAN, ROWS, LANES), jnp.bfloat16),
        scratch_shapes=[pltpu.VMEM((COLUMNS, 4 * LANES), jnp.bfloat16)],
        compiler_params=limit(16),
        cost_estimate=pl.CostEstimate(
            flops=2 * 2048 * 512 * 192, bytes_accessed=3 << 20, transcendentals=0
        ),
        name="cross_full",
    )(owners, got)


def mid_kernel(core, got, own, other, partial, out, columns):
    del partial
    first = core[0] == 0
    planned = []
    for s in range(STEPS):
        mine, theirs = own[s], other[s]
        low, high = jnp.where(first, mine, theirs), jnp.where(first, theirs, mine)
        planned.append(jnp.concatenate([low, high], axis=2))
    columns[...] = planned_columns(planned)
    for start in range(0, N_CHAN, 16):
        left = got[start : start + 16, :, :, 32:48, :]
        out[start : start + 16, FULL_ROWS:, :] = packed(products(left, columns[...]))


def cross_mid(core, got, own, other, partial):
    return pl.pallas_call(
        mid_kernel,
        in_specs=[pl.BlockSpec(memory_space=pltpu.SMEM)] + [vmem()] * 4,
        out_specs=vmem(),
        out_shape=jax.ShapeDtypeStruct((N_CHAN, ROWS, LANES), jnp.bfloat16),
        scratch_shapes=[pltpu.VMEM((COLUMNS, 4 * LANES), jnp.bfloat16)],
        input_output_aliases={4: 0},
        compiler_params=limit(16),
        cost_estimate=pl.CostEstimate(
            flops=2 * 1024 * 512 * 192, bytes_accessed=2 << 20, transcendentals=0
        ),
        name="cross_mid",
    )(core, got, own, other, partial)


def order_kernel(back, out):
    g = pl.program_id(0)
    first = pl.multiple_of(16 * g, 16)

    def turned(full, mid):
        return jnp.concatenate([full, mid], axis=0).T

    full = jnp.swapaxes(back[:, :, pl.ds(first, 16), :].reshape(N_CHAN, 16, LANES), 0, 1)
    mid = jnp.swapaxes(back[:, g, 48:64, :], 0, 1)
    for c in range(16):
        columns = turned(full[c], mid[c])
        for u in range(4):
            out[u // STEPS, u % STEPS, c] = columns[32 * u : 32 * u + 32]
    rest = back[:, :, 32:48, :].reshape(N_CHAN, 16, LANES).astype(jnp.float32)
    rest = jnp.where(g == 0, rest[:, :8], rest[:, 8:])
    rest = jnp.swapaxes(rest, 0, 1).astype(jnp.bfloat16)
    mid = jnp.swapaxes(back[:, g, 64:72, :].astype(jnp.float32), 0, 1).astype(jnp.bfloat16)
    for e in range(8):
        columns = turned(rest[e], mid[e])
        for half in range(2):
            for u in (4, 5):
                start = 64 * half + 32 * (u - 4)
                out[u // STEPS, u % STEPS, e + 8 * half] = columns[start : start + 32]


def ordered(back):
    return pl.pallas_call(
        order_kernel,
        grid=(2,),
        in_specs=[vmem()],
        out_specs=pl.BlockSpec((2, STEPS, 16, 32, 96), lambda g: (0, 0, g, 0, 0)),
        out_shape=jax.ShapeDtypeStruct((2, STEPS, 32, 32, 96), jnp.bfloat16),
        compiler_params=limit(24),
        cost_estimate=pl.CostEstimate(flops=0, bytes_accessed=4 << 20, transcendentals=0),
        name="order",
    )(back.reshape(32, 2, ROWS, LANES))


def per_device(signal, valid, owners):
    got = lax.all_to_all(
        whitened(signal, valid).reshape(128, 2, 48, LANES), ("chan", "win"), 0, 0, tiled=True
    ).reshape(N_CHAN, 2, 2, 48, LANES)
    own = picked(owners, got)
    other = lax.ppermute(own, "chan", [(i, i ^ 1) for i in range(N_CHAN)])
    core = (lax.axis_index("chan") & 1).reshape(1)
    result = cross_mid(core, got, own, other, cross_full(owners, got))
    back = lax.all_to_all(result, "chan", 0, 0, tiled=True)
    return jnp.transpose(ordered(back), (0, 1, 4, 2, 3))


def solution(mesh):
    in_specs = (P("chan", "win", None), P("chan", "win"), P())
    out_specs = P(None, None, "win", "chan", None)
    return jax.shard_map(
        per_device, mesh=mesh, in_specs=in_specs, out_specs=out_specs, check_vma=False
    )
```

```python
import math

import jax
import jax.numpy as jnp
from jax import lax
from jax.experimental import pallas as pl
from jax.experimental.pallas import tpu as pltpu
from jax.sharding import PartitionSpec as P

SAMPLES = 1024
BINS = 192
WINDOWS = 256
STEPS = 3
CH_DEV = 32
N_CHAN = 64
LANES = 128
COLUMNS = 2 * STEPS * CH_DEV
FULL_ROWS, ROWS = 48, 72
CHUNKS = ((0, 4), (4, 12), (12, 32))


def vmem():
    return pl.BlockSpec(memory_space=pltpu.VMEM)


def limit(mib):
    return pltpu.CompilerParams(vmem_limit_bytes=mib << 20)


def angles(rows, scale):
    times = lax.broadcasted_iota(jnp.int32, (rows, SAMPLES), 1)
    freqs = lax.broadcasted_iota(jnp.int32, (rows, SAMPLES), 0) * scale
    return (freqs * times % SAMPLES).astype(jnp.float32) * (2.0 * math.pi / SAMPLES)


def fill_table(table):
    fine = angles(32, 1)
    coarse = angles(8, 32)
    times = lax.broadcasted_iota(jnp.int32, (1, SAMPLES), 1).astype(jnp.float32)
    taper = 0.5 - 0.5 * jnp.cos(times * (2.0 * math.pi / SAMPLES))
    fine_cos, fine_sin = jnp.cos(fine) * taper, jnp.sin(fine) * taper
    coarse_cos, coarse_sin = jnp.cos(coarse), jnp.sin(coarse)
    for a in range(6):
        cos_a, sin_a = coarse_cos[a + 1 : a + 2], coarse_sin[a + 1 : a + 2]
        real = cos_a * fine_cos - sin_a * fine_sin
        imag = -sin_a * fine_cos - cos_a * fine_sin
        table[32 * a : 32 * a + 32, :] = real.astype(jnp.bfloat16)
        table[BINS + 32 * a : BINS + 32 * a + 32, :] = imag.astype(jnp.bfloat16)


def whiten_kernel(signal, valid, white, samples, usable, table, sems):
    copies = [pltpu.make_async_copy(valid, usable, sems.at[len(CHUNKS)])]
    for k, (start, end) in enumerate(CHUNKS):
        copies.append(
            pltpu.make_async_copy(signal.at[start:end], samples.at[start:end], sems.at[k])
        )
    for copy in copies:
        copy.start()
    fill_table(table)
    copies[0].wait()
    weights = usable[...].astype(jnp.float32)
    arrives = {start: copy for (start, _), copy in zip(CHUNKS, copies[1:])}
    for c0 in range(0, CH_DEV, 2):
        if c0 in arrives:
            arrives[c0].wait()
        both = samples[c0 : c0 + 2].reshape(2 * LANES, SAMPLES)
        spec = lax.dot_general(
            table[...], both, (((1,), (1,)), ((), ())), preferred_element_type=jnp.float32
        )
        power = jnp.sum(spec * spec, axis=0, keepdims=True) * (1.0 / BINS)
        factor = lax.rsqrt(power + 1e-06)
        for one in range(2):
            lanes = slice(one * LANES, (one + 1) * LANES)
            scale = factor[:, lanes] * weights[c0 + one : c0 + one + 1, :]
            white[c0 + one] = (spec[:, lanes] * scale).astype(jnp.bfloat16)


def whitened(signal, valid):
    signal = pltpu.with_memory_space_constraint(signal, pltpu.HBM)
    valid = pltpu.with_memory_space_constraint(valid, pltpu.HBM)
    return pl.pallas_call(
        whiten_kernel,
        in_specs=[pl.BlockSpec(memory_space=pltpu.HBM)] * 2,
        out_specs=vmem(),
        out_shape=jax.ShapeDtypeStruct((CH_DEV, 2 * BINS, LANES), jnp.bfloat16),
        scratch_shapes=[
            pltpu.VMEM((CH_DEV, LANES, SAMPLES), jnp.bfloat16),
            pltpu.VMEM((CH_DEV, LANES), jnp.int32),
            pltpu.VMEM((2 * BINS, SAMPLES), jnp.bfloat16),
            pltpu.SemaphoreType.DMA((len(CHUNKS) + 1,)),
        ],
        compiler_params=limit(40),
        cost_estimate=pl.CostEstimate(
            flops=2 * 2 * BINS * SAMPLES * 4096, bytes_accessed=12 << 20, transcendentals=0
        ),
        name="whiten",
    )(signal, valid)


def place_kernel(white, out):
    for g in range(2):
        c = slice(16 * g, 16 * g + 16)
        for h in range(2):
            for r in range(2):
                for m in range(3):
                    start = BINS * r + 96 * h + 32 * m
                    rows = jnp.swapaxes(white[c, start : start + 32, :], 0, 1)
                    if m == 2:
                        out[:, g, h, r, 32:48, :] = rows
                    else:
                        to = slice(16 * m, 16 * m + 16)
                        out[to, :, h, r, c, :] = rows.reshape(16, 2, 16, LANES)


def placed(white):
    return pl.pallas_call(
        place_kernel,
        in_specs=[vmem()],
        out_specs=vmem(),
        out_shape=jax.ShapeDtypeStruct((32, 2, 2, 2, 48, LANES), jnp.bfloat16),
        compiler_params=limit(16),
        cost_estimate=pl.CostEstimate(flops=0, bytes_accessed=6 << 20, transcendentals=0),
        name="place",
    )(white)


def pick_kernel(owners, got, out):
    for s in range(STEPS):
        out[s] = got[owners[s], :, :, 32:48, :]


def picked(owners, got):
    return pl.pallas_call(
        pick_kernel,
        in_specs=[pl.BlockSpec(memory_space=pltpu.SMEM), vmem()],
        out_specs=vmem(),
        out_shape=jax.ShapeDtypeStruct((STEPS, 2, 2, 16, LANES), jnp.bfloat16),
        compiler_params=limit(16),
        cost_estimate=pl.CostEstimate(flops=0, bytes_accessed=98304, transcendentals=0),
        name="pick",
    )(owners, got)


def planned_columns(planned):
    real = [jnp.concatenate([b[0, 0], b[0, 1], b[1, 0], b[1, 1]], axis=1) for b in planned]
    imag = [jnp.concatenate([-b[0, 1], b[0, 0], -b[1, 1], b[1, 0]], axis=1) for b in planned]
    return jnp.concatenate(real + imag, axis=0)


def products(left, columns):
    count, channels = left.shape[0], left.shape[3]
    rows = jnp.concatenate(
        [left[:, w, r].reshape(count * channels, LANES) for w in range(2) for r in range(2)], axis=1
    )
    result = lax.dot_general(
        rows, columns, (((1,), (1,)), ((), ())), preferred_element_type=jnp.float32
    )
    return (result * (1.0 / math.sqrt(WINDOWS))).reshape(count, channels, COLUMNS)


def packed(result):
    rest = result[:, :, LANES:]
    parts = [result[:, :, :LANES]]
    for start in range(0, result.shape[1], 16):
        parts.append(
            jnp.concatenate([rest[:, start : start + 8], rest[:, start + 8 : start + 16]], axis=2)
        )
    return jnp.concatenate(parts, axis=1).astype(jnp.bfloat16)


def full_kernel(owners, got, out, columns):
    columns[...] = planned_columns([got[owners[s], :, :, :32, :] for s in range(STEPS)])
    for start in range(0, N_CHAN, 8):
        left = got[start : start + 8, :, :, :32, :]
        out[start : start + 8, :FULL_ROWS, :] = packed(products(left, columns[...]))


def cross_full(owners, got):
    return pl.pallas_call(
        full_kernel,
        in_specs=[pl.BlockSpec(memory_space=pltpu.SMEM), vmem()],
        out_specs=vmem(),
        out_shape=jax.ShapeDtypeStruct((N_CHAN, ROWS, LANES), jnp.bfloat16),
        scratch_shapes=[pltpu.VMEM((COLUMNS, 4 * LANES), jnp.bfloat16)],
        compiler_params=limit(16),
        cost_estimate=pl.CostEstimate(
            flops=2 * 2048 * 512 * 192, bytes_accessed=3 << 20, transcendentals=0
        ),
        name="cross_full",
    )(owners, got)


def mid_kernel(core, got, own, other, partial, out, columns):
    del partial
    first = core[0] == 0
    planned = []
    for s in range(STEPS):
        mine, theirs = own[s], other[s]
        low, high = jnp.where(first, mine, theirs), jnp.where(first, theirs, mine)
        planned.append(jnp.concatenate([low, high], axis=2))
    columns[...] = planned_columns(planned)
    for start in range(0, N_CHAN, 16):
        left = got[start : start + 16, :, :, 32:48, :]
        out[start : start + 16, FULL_ROWS:, :] = packed(products(left, columns[...]))


def cross_mid(core, got, own, other, partial):
    return pl.pallas_call(
        mid_kernel,
        in_specs=[pl.BlockSpec(memory_space=pltpu.SMEM)] + [vmem()] * 4,
        out_specs=vmem(),
        out_shape=jax.ShapeDtypeStruct((N_CHAN, ROWS, LANES), jnp.bfloat16),
        scratch_shapes=[pltpu.VMEM((COLUMNS, 4 * LANES), jnp.bfloat16)],
        input_output_aliases={4: 0},
        compiler_params=limit(16),
        cost_estimate=pl.CostEstimate(
            flops=2 * 1024 * 512 * 192, bytes_accessed=2 << 20, transcendentals=0
        ),
        name="cross_mid",
    )(core, got, own, other, partial)


def order_kernel(back, out):
    g = pl.program_id(0)
    first = pl.multiple_of(16 * g, 16)

    def turned(full, mid):
        return jnp.concatenate([full, mid], axis=0).T

    full = jnp.swapaxes(back[:, :, pl.ds(first, 16), :].reshape(N_CHAN, 16, LANES), 0, 1)
    mid = jnp.swapaxes(back[:, g, 48:64, :], 0, 1)
    for c in range(16):
        columns = turned(full[c], mid[c])
        for u in range(4):
            out[u // STEPS, u % STEPS, c] = columns[32 * u : 32 * u + 32]
    rest = back[:, :, 32:48, :].reshape(N_CHAN, 16, LANES).astype(jnp.float32)
    rest = jnp.where(g == 0, rest[:, :8], rest[:, 8:])
    rest = jnp.swapaxes(rest, 0, 1).astype(jnp.bfloat16)
    mid = jnp.swapaxes(back[:, g, 64:72, :].astype(jnp.float32), 0, 1).astype(jnp.bfloat16)
    for e in range(8):
        columns = turned(rest[e], mid[e])
        for half in range(2):
            for u in (4, 5):
                start = 64 * half + 32 * (u - 4)
                out[u // STEPS, u % STEPS, e + 8 * half] = columns[start : start + 32]


def ordered(back):
    return pl.pallas_call(
        order_kernel,
        grid=(2,),
        in_specs=[vmem()],
        out_specs=pl.BlockSpec((2, STEPS, 16, 32, 96), lambda g: (0, 0, g, 0, 0)),
        out_shape=jax.ShapeDtypeStruct((2, STEPS, 32, 32, 96), jnp.bfloat16),
        compiler_params=limit(24),
        cost_estimate=pl.CostEstimate(flops=0, bytes_accessed=4 << 20, transcendentals=0),
        name="order",
    )(back.reshape(32, 2, ROWS, LANES))


def per_device(signal, valid, owners):
    got = lax.all_to_all(
        placed(whitened(signal, valid)).reshape(128, 2, 48, LANES), ("chan", "win"), 0, 0, tiled=True
    ).reshape(N_CHAN, 2, 2, 48, LANES)
    own = picked(owners, got)
    other = lax.ppermute(own, "chan", [(i, i ^ 1) for i in range(N_CHAN)])
    core = (lax.axis_index("chan") & 1).reshape(1)
    result = cross_mid(core, got, own, other, cross_full(owners, got))
    back = lax.all_to_all(result, "chan", 0, 0, tiled=True)
    return jnp.transpose(ordered(back), (0, 1, 4, 2, 3))


def solution(mesh):
    in_specs = (P("chan", "win", None), P("chan", "win"), P())
    out_specs = P(None, None, "win", "chan", None)
    return jax.shard_map(
        per_device, mesh=mesh, in_specs=in_specs, out_specs=out_specs, check_vma=False
    )
```

```python
import math

import jax
import jax.numpy as jnp
from jax import lax
from jax.experimental import pallas as pl
from jax.experimental.pallas import tpu as pltpu
from jax.sharding import PartitionSpec as P

SAMPLES = 1024
BINS = 192
WINDOWS = 256
STEPS = 3
CH_DEV = 32
N_CHAN = 64
LANES = 128
COLUMNS = 2 * STEPS * CH_DEV
FULL_ROWS, ROWS = 48, 72
CHUNKS = ((0, 4), (4, 12), (12, 32))


def vmem():
    return pl.BlockSpec(memory_space=pltpu.VMEM)


def limit(mib):
    return pltpu.CompilerParams(vmem_limit_bytes=mib << 20)


def angles(rows, scale):
    times = lax.broadcasted_iota(jnp.int32, (rows, SAMPLES), 1)
    freqs = lax.broadcasted_iota(jnp.int32, (rows, SAMPLES), 0) * scale
    return (freqs * times % SAMPLES).astype(jnp.float32) * (2.0 * math.pi / SAMPLES)


def fill_table(table):
    fine = angles(32, 1)
    coarse = angles(8, 32)
    times = lax.broadcasted_iota(jnp.int32, (1, SAMPLES), 1).astype(jnp.float32)
    taper = 0.5 - 0.5 * jnp.cos(times * (2.0 * math.pi / SAMPLES))
    fine_cos, fine_sin = jnp.cos(fine) * taper, jnp.sin(fine) * taper
    coarse_cos, coarse_sin = jnp.cos(coarse), jnp.sin(coarse)
    for a in range(6):
        cos_a, sin_a = coarse_cos[a + 1 : a + 2], coarse_sin[a + 1 : a + 2]
        real = cos_a * fine_cos - sin_a * fine_sin
        imag = -sin_a * fine_cos - cos_a * fine_sin
        table[32 * a : 32 * a + 32, :] = real.astype(jnp.bfloat16)
        table[BINS + 32 * a : BINS + 32 * a + 32, :] = imag.astype(jnp.bfloat16)


def whiten_kernel(signal, valid, white, samples, usable, table, sems):
    copies = [pltpu.make_async_copy(valid, usable, sems.at[len(CHUNKS)])]
    for k, (start, end) in enumerate(CHUNKS):
        copies.append(
            pltpu.make_async_copy(signal.at[start:end], samples.at[start:end], sems.at[k])
        )
    for copy in copies:
        copy.start()
    fill_table(table)
    copies[0].wait()
    weights = usable[...].astype(jnp.float32)
    arrives = {start: copy for (start, _), copy in zip(CHUNKS, copies[1:])}
    for c0 in range(0, CH_DEV, 2):
        if c0 in arrives:
            arrives[c0].wait()
        both = samples[c0 : c0 + 2].reshape(2 * LANES, SAMPLES)
        spec = lax.dot_general(
            table[...], both, (((1,), (1,)), ((), ())), preferred_element_type=jnp.float32
        )
        power = jnp.sum(spec * spec, axis=0, keepdims=True) * (1.0 / BINS)
        factor = lax.rsqrt(power + 1e-06)
        for one in range(2):
            lanes = slice(one * LANES, (one + 1) * LANES)
            scale = factor[:, lanes] * weights[c0 + one : c0 + one + 1, :]
            white[c0 + one] = (spec[:, lanes] * scale).astype(jnp.bfloat16)


def whitened(signal, valid):
    signal = pltpu.with_memory_space_constraint(signal, pltpu.HBM)
    valid = pltpu.with_memory_space_constraint(valid, pltpu.HBM)
    return pl.pallas_call(
        whiten_kernel,
        in_specs=[pl.BlockSpec(memory_space=pltpu.HBM)] * 2,
        out_specs=vmem(),
        out_shape=jax.ShapeDtypeStruct((CH_DEV, 2 * BINS, LANES), jnp.bfloat16),
        scratch_shapes=[
            pltpu.VMEM((CH_DEV, LANES, SAMPLES), jnp.bfloat16),
            pltpu.VMEM((CH_DEV, LANES), jnp.int32),
            pltpu.VMEM((2 * BINS, SAMPLES), jnp.bfloat16),
            pltpu.SemaphoreType.DMA((len(CHUNKS) + 1,)),
        ],
        compiler_params=limit(40),
        cost_estimate=pl.CostEstimate(
            flops=2 * 2 * BINS * SAMPLES * 4096, bytes_accessed=12 << 20, transcendentals=0
        ),
        name="whiten",
    )(signal, valid)


def place_kernel(white, out):
    for g in range(2):
        c = slice(16 * g, 16 * g + 16)
        for h in range(2):
            for r in range(2):
                for m in range(3):
                    start = BINS * r + 96 * h + 32 * m
                    rows = jnp.swapaxes(white[c, start : start + 32, :], 0, 1)
                    if m == 2:
                        out[:, g, h, r, 32:48, :] = rows
                    else:
                        to = slice(16 * m, 16 * m + 16)
                        out[to, :, h, r, c, :] = rows.reshape(16, 2, 16, LANES)


def placed(white):
    return pl.pallas_call(
        place_kernel,
        in_specs=[vmem()],
        out_specs=vmem(),
        out_shape=jax.ShapeDtypeStruct((32, 2, 2, 2, 48, LANES), jnp.bfloat16),
        compiler_params=limit(16),
        cost_estimate=pl.CostEstimate(flops=0, bytes_accessed=6 << 20, transcendentals=0),
        name="place",
    )(white)


def planned_columns(planned):
    real = [jnp.concatenate([b[0, 0], b[0, 1], b[1, 0], b[1, 1]], axis=1) for b in planned]
    imag = [jnp.concatenate([-b[0, 1], b[0, 0], -b[1, 1], b[1, 0]], axis=1) for b in planned]
    return jnp.concatenate(real + imag, axis=0)


def pick_kernel(owners, got, own, columns):
    planned = []
    for s in range(STEPS):
        owner = owners[s]
        own[s] = got[owner, :, :, 32:48, :]
        planned.append(got[owner, :, :, :32, :])
    columns[...] = planned_columns(planned)


def picked(owners, got):
    return pl.pallas_call(
        pick_kernel,
        in_specs=[pl.BlockSpec(memory_space=pltpu.SMEM), vmem()],
        out_specs=[vmem(), vmem()],
        out_shape=[
            jax.ShapeDtypeStruct((STEPS, 2, 2, 16, LANES), jnp.bfloat16),
            jax.ShapeDtypeStruct((COLUMNS, 4 * LANES), jnp.bfloat16),
        ],
        compiler_params=limit(16),
        cost_estimate=pl.CostEstimate(flops=0, bytes_accessed=98304, transcendentals=0),
        name="pick",
    )(owners, got)


def products(left, columns):
    count, channels = left.shape[0], left.shape[3]
    rows = jnp.concatenate(
        [left[:, w, r].reshape(count * channels, LANES) for w in range(2) for r in range(2)], axis=1
    )
    result = lax.dot_general(
        rows, columns, (((1,), (1,)), ((), ())), preferred_element_type=jnp.float32
    )
    return (result * (1.0 / math.sqrt(WINDOWS))).reshape(count, channels, COLUMNS)


def packed(result):
    rest = result[:, :, LANES:]
    parts = [result[:, :, :LANES]]
    for start in range(0, result.shape[1], 16):
        parts.append(
            jnp.concatenate([rest[:, start : start + 8], rest[:, start + 8 : start + 16]], axis=2)
        )
    return jnp.concatenate(parts, axis=1).astype(jnp.bfloat16)


def full_kernel(got, columns, out):
    for start in range(0, N_CHAN, 8):
        left = got[start : start + 8, :, :, :32, :]
        out[start : start + 8, :FULL_ROWS, :] = packed(products(left, columns[...]))


def cross_full(got, columns):
    return pl.pallas_call(
        full_kernel,
        in_specs=[vmem(), vmem()],
        out_specs=vmem(),
        out_shape=jax.ShapeDtypeStruct((N_CHAN, ROWS, LANES), jnp.bfloat16),
        compiler_params=limit(16),
        cost_estimate=pl.CostEstimate(
            flops=2 * 2048 * 512 * 192, bytes_accessed=3 << 20, transcendentals=0
        ),
        name="cross_full",
    )(got, columns)


def mid_kernel(got, own, other, partial, out, columns):
    del partial
    first = (lax.axis_index("chan") & 1) == 0
    planned = []
    for s in range(STEPS):
        mine, theirs = own[s], other[s]
        low, high = jnp.where(first, mine, theirs), jnp.where(first, theirs, mine)
        planned.append(jnp.concatenate([low, high], axis=2))
    columns[...] = planned_columns(planned)
    for start in range(0, N_CHAN, 16):
        left = got[start : start + 16, :, :, 32:48, :]
        out[start : start + 16, FULL_ROWS:, :] = packed(products(left, columns[...]))


def cross_mid(got, own, other, partial):
    return pl.pallas_call(
        mid_kernel,
        in_specs=[vmem()] * 4,
        out_specs=vmem(),
        out_shape=jax.ShapeDtypeStruct((N_CHAN, ROWS, LANES), jnp.bfloat16),
        scratch_shapes=[pltpu.VMEM((COLUMNS, 4 * LANES), jnp.bfloat16)],
        input_output_aliases={3: 0},
        compiler_params=limit(16),
        cost_estimate=pl.CostEstimate(
            flops=2 * 1024 * 512 * 192, bytes_accessed=2 << 20, transcendentals=0
        ),
        name="cross_mid",
    )(got, own, other, partial)


def order_kernel(back, out):
    g = pl.program_id(0)
    first = pl.multiple_of(16 * g, 16)

    def turned(full, mid):
        return jnp.concatenate([full, mid], axis=0).T

    full = jnp.swapaxes(back[:, :, pl.ds(first, 16), :].reshape(N_CHAN, 16, LANES), 0, 1)
    mid = jnp.swapaxes(back[:, g, 48:64, :], 0, 1)
    for c in range(16):
        columns = turned(full[c], mid[c])
        for u in range(4):
            out[u // STEPS, u % STEPS, c] = columns[32 * u : 32 * u + 32]
    rest = back[:, :, 32:48, :].reshape(N_CHAN, 16, LANES).astype(jnp.float32)
    rest = jnp.where(g == 0, rest[:, :8], rest[:, 8:])
    rest = jnp.swapaxes(rest, 0, 1).astype(jnp.bfloat16)
    mid = jnp.swapaxes(back[:, g, 64:72, :].astype(jnp.float32), 0, 1).astype(jnp.bfloat16)
    for e in range(8):
        columns = turned(rest[e], mid[e])
        for half in range(2):
            for u in (4, 5):
                start = 64 * half + 32 * (u - 4)
                out[u // STEPS, u % STEPS, e + 8 * half] = columns[start : start + 32]


def ordered(back):
    return pl.pallas_call(
        order_kernel,
        grid=(2,),
        in_specs=[vmem()],
        out_specs=pl.BlockSpec((2, STEPS, 16, 32, 96), lambda g: (0, 0, g, 0, 0)),
        out_shape=jax.ShapeDtypeStruct((2, STEPS, 32, 32, 96), jnp.bfloat16),
        compiler_params=limit(24),
        cost_estimate=pl.CostEstimate(flops=0, bytes_accessed=4 << 20, transcendentals=0),
        name="order",
    )(back.reshape(32, 2, ROWS, LANES))


def per_device(signal, valid, owners):
    got = lax.all_to_all(
        placed(whitened(signal, valid)).reshape(128, 2, 48, LANES), ("chan", "win"), 0, 0, tiled=True
    ).reshape(N_CHAN, 2, 2, 48, LANES)
    own, columns = picked(owners, got)
    other = lax.ppermute(own, "chan", [(i, i ^ 1) for i in range(N_CHAN)])
    result = cross_mid(got, own, other, cross_full(got, columns))
    back = lax.all_to_all(result, "chan", 0, 0, tiled=True)
    return jnp.transpose(ordered(back), (0, 1, 4, 2, 3))


def solution(mesh):
    in_specs = (P("chan", "win", None), P("chan", "win"), P())
    out_specs = P(None, None, "win", "chan", None)
    return jax.shard_map(
        per_device, mesh=mesh, in_specs=in_specs, out_specs=out_specs, check_vma=False
    )
```

```python
import math

import jax
import jax.numpy as jnp
from jax import lax
from jax.experimental import pallas as pl
from jax.experimental.pallas import tpu as pltpu
from jax.sharding import Mesh
from jax.sharding import PartitionSpec as P

SAMPLES = 1024
BINS = 192
WINDOWS = 256
STEPS = 3
CH_DEV = 32
N_CHAN = 64
LANES = 128
COLUMNS = 2 * STEPS * CH_DEV
FULL_ROWS, ROWS = 48, 72
CHUNKS = ((0, 4), (4, 12), (12, 32))


def vmem():
    return pl.BlockSpec(memory_space=pltpu.VMEM)


def limit(mib):
    return pltpu.CompilerParams(vmem_limit_bytes=mib << 20)


def angles(rows, scale):
    times = lax.broadcasted_iota(jnp.int32, (rows, SAMPLES), 1)
    freqs = lax.broadcasted_iota(jnp.int32, (rows, SAMPLES), 0) * scale
    return (freqs * times % SAMPLES).astype(jnp.float32) * (2.0 * math.pi / SAMPLES)


def fill_table(table):
    fine = angles(32, 1)
    coarse = angles(8, 32)
    times = lax.broadcasted_iota(jnp.int32, (1, SAMPLES), 1).astype(jnp.float32)
    taper = 0.5 - 0.5 * jnp.cos(times * (2.0 * math.pi / SAMPLES))
    fine_cos, fine_sin = jnp.cos(fine) * taper, jnp.sin(fine) * taper
    coarse_cos, coarse_sin = jnp.cos(coarse), jnp.sin(coarse)
    for a in range(6):
        cos_a, sin_a = coarse_cos[a + 1 : a + 2], coarse_sin[a + 1 : a + 2]
        real = cos_a * fine_cos - sin_a * fine_sin
        imag = -sin_a * fine_cos - cos_a * fine_sin
        table[32 * a : 32 * a + 32, :] = real.astype(jnp.bfloat16)
        table[BINS + 32 * a : BINS + 32 * a + 32, :] = imag.astype(jnp.bfloat16)


def whiten_kernel(signal, valid, white, samples, usable, table, sems):
    copies = [pltpu.make_async_copy(valid, usable, sems.at[len(CHUNKS)])]
    for k, (start, end) in enumerate(CHUNKS):
        copies.append(
            pltpu.make_async_copy(signal.at[start:end], samples.at[start:end], sems.at[k])
        )
    for copy in copies:
        copy.start()
    fill_table(table)
    copies[0].wait()
    weights = usable[...].astype(jnp.float32)
    arrives = {start: copy for (start, _), copy in zip(CHUNKS, copies[1:])}
    for c0 in range(0, CH_DEV, 2):
        if c0 in arrives:
            arrives[c0].wait()
        both = samples[c0 : c0 + 2].reshape(2 * LANES, SAMPLES)
        spec = lax.dot_general(
            table[...], both, (((1,), (1,)), ((), ())), preferred_element_type=jnp.float32
        )
        power = jnp.sum(spec * spec, axis=0, keepdims=True) * (1.0 / BINS)
        factor = lax.rsqrt(power + 1e-06)
        for one in range(2):
            lanes = slice(one * LANES, (one + 1) * LANES)
            scale = factor[:, lanes] * weights[c0 + one : c0 + one + 1, :]
            white[c0 + one] = (spec[:, lanes] * scale).astype(jnp.bfloat16)


def whitened(signal, valid):
    signal = pltpu.with_memory_space_constraint(signal, pltpu.HBM)
    valid = pltpu.with_memory_space_constraint(valid, pltpu.HBM)
    return pl.pallas_call(
        whiten_kernel,
        in_specs=[pl.BlockSpec(memory_space=pltpu.HBM)] * 2,
        out_specs=vmem(),
        out_shape=jax.ShapeDtypeStruct((CH_DEV, 2 * BINS, LANES), jnp.bfloat16),
        scratch_shapes=[
            pltpu.VMEM((CH_DEV, LANES, SAMPLES), jnp.bfloat16),
            pltpu.VMEM((CH_DEV, LANES), jnp.int32),
            pltpu.VMEM((2 * BINS, SAMPLES), jnp.bfloat16),
            pltpu.SemaphoreType.DMA((len(CHUNKS) + 1,)),
        ],
        compiler_params=limit(40),
        cost_estimate=pl.CostEstimate(
            flops=2 * 2 * BINS * SAMPLES * 4096, bytes_accessed=12 << 20, transcendentals=0
        ),
        name="whiten",
    )(signal, valid)


def place_kernel(white, out):
    for g in range(2):
        c = slice(16 * g, 16 * g + 16)
        for h in range(2):
            for r in range(2):
                for m in range(3):
                    start = BINS * r + 96 * h + 32 * m
                    rows = jnp.swapaxes(white[c, start : start + 32, :], 0, 1)
                    rows = rows.reshape(2, 16, 16, LANES)
                    if m == 2:
                        out[:, h, g, :, r, 32:48, :] = rows
                    else:
                        out[m, h, :, :, r, c, :] = rows


def placed(white):
    return pl.pallas_call(
        place_kernel,
        in_specs=[vmem()],
        out_specs=vmem(),
        out_shape=jax.ShapeDtypeStruct((2, 2, 2, 16, 2, 48, LANES), jnp.bfloat16),
        compiler_params=limit(16),
        cost_estimate=pl.CostEstimate(flops=0, bytes_accessed=6 << 20, transcendentals=0),
        name="place",
    )(white)


def planned_columns(planned):
    real = [jnp.concatenate([b[0, 0], b[0, 1], b[1, 0], b[1, 1]], axis=1) for b in planned]
    imag = [jnp.concatenate([-b[0, 1], b[0, 0], -b[1, 1], b[1, 0]], axis=1) for b in planned]
    return jnp.concatenate(real + imag, axis=0)


def pick_kernel(owners, got, own, columns):
    planned = []
    for s in range(STEPS):
        owner = owners[s]
        y, x = lax.shift_right_logical(owner, 4), lax.shift_right_logical(owner, 2) & 3
        zh, core = lax.shift_right_logical(owner, 1) & 1, owner & 1
        at = core * 16 + x * 4 + y
        own[s] = got[zh, :, at, :, 32:48, :]
        planned.append(got[zh, :, at, :, :32, :])
    columns[...] = planned_columns(planned)


def picked(owners, got):
    return pl.pallas_call(
        pick_kernel,
        in_specs=[pl.BlockSpec(memory_space=pltpu.SMEM), vmem()],
        out_specs=[vmem(), vmem()],
        out_shape=[
            jax.ShapeDtypeStruct((STEPS, 2, 2, 16, LANES), jnp.bfloat16),
            jax.ShapeDtypeStruct((COLUMNS, 4 * LANES), jnp.bfloat16),
        ],
        compiler_params=limit(16),
        cost_estimate=pl.CostEstimate(flops=0, bytes_accessed=98304, transcendentals=0),
        name="pick",
    )(owners, got)


def products(left, columns):
    count, channels = left.shape[1], left.shape[3]
    rows = jnp.concatenate(
        [left[w, :, r].reshape(count * channels, LANES) for w in range(2) for r in range(2)], axis=1
    )
    result = lax.dot_general(
        rows, columns, (((1,), (1,)), ((), ())), preferred_element_type=jnp.float32
    )
    return (result * (1.0 / math.sqrt(WINDOWS))).reshape(count, channels, COLUMNS)


def packed(result):
    rest = result[:, :, LANES:]
    parts = [result[:, :, :LANES]]
    for start in range(0, result.shape[1], 16):
        parts.append(
            jnp.concatenate([rest[:, start : start + 8], rest[:, start + 8 : start + 16]], axis=2)
        )
    return jnp.concatenate(parts, axis=1).astype(jnp.bfloat16)


def full_kernel(got, columns, out):
    for start in range(0, N_CHAN, 8):
        zh, at = divmod(start, 32)
        left = got[zh, :, at : at + 8, :, :32, :]
        out[start : start + 8, :FULL_ROWS, :] = packed(products(left, columns[...]))


def cross_full(got, columns):
    return pl.pallas_call(
        full_kernel,
        in_specs=[vmem(), vmem()],
        out_specs=vmem(),
        out_shape=jax.ShapeDtypeStruct((N_CHAN, ROWS, LANES), jnp.bfloat16),
        compiler_params=limit(16),
        cost_estimate=pl.CostEstimate(
            flops=2 * 2048 * 512 * 192, bytes_accessed=3 << 20, transcendentals=0
        ),
        name="cross_full",
    )(got, columns)


def mid_kernel(got, own, other, partial, out, columns):
    del partial
    first = lax.axis_index("core") == 0
    planned = []
    for s in range(STEPS):
        mine, theirs = own[s], other[s]
        low, high = jnp.where(first, mine, theirs), jnp.where(first, theirs, mine)
        planned.append(jnp.concatenate([low, high], axis=2))
    columns[...] = planned_columns(planned)
    for start in range(0, N_CHAN, 16):
        zh, at = divmod(start, 32)
        left = got[zh, :, at : at + 16, :, 32:48, :]
        out[start : start + 16, FULL_ROWS:, :] = packed(products(left, columns[...]))


def cross_mid(got, own, other, partial):
    return pl.pallas_call(
        mid_kernel,
        in_specs=[vmem()] * 4,
        out_specs=vmem(),
        out_shape=jax.ShapeDtypeStruct((N_CHAN, ROWS, LANES), jnp.bfloat16),
        scratch_shapes=[pltpu.VMEM((COLUMNS, 4 * LANES), jnp.bfloat16)],
        input_output_aliases={3: 0},
        compiler_params=limit(16),
        cost_estimate=pl.CostEstimate(
            flops=2 * 1024 * 512 * 192, bytes_accessed=2 << 20, transcendentals=0
        ),
        name="cross_mid",
    )(got, own, other, partial)


def order_kernel(back, out):
    g = pl.program_id(0)
    first = pl.multiple_of(16 * g, 16)

    def turned(full, mid):
        return jnp.concatenate([full, mid], axis=0).T

    full = jnp.swapaxes(back[:, :, :, pl.ds(first, 16), :].reshape(N_CHAN, 16, LANES), 0, 1)
    mid = jnp.swapaxes(back[:, g, :, 48:64, :].reshape(32, 16, LANES), 0, 1)
    for c in range(16):
        columns = turned(full[c], mid[c])
        for u in range(4):
            out[u // STEPS, u % STEPS, c] = columns[32 * u : 32 * u + 32]
    rest = back[:, :, :, 32:48, :].reshape(N_CHAN, 16, LANES).astype(jnp.float32)
    rest = jnp.where(g == 0, rest[:, :8], rest[:, 8:])
    rest = jnp.swapaxes(rest, 0, 1).astype(jnp.bfloat16)
    mid = back[:, g, :, 64:72, :].astype(jnp.float32).reshape(32, 8, LANES)
    mid = jnp.swapaxes(mid, 0, 1).astype(jnp.bfloat16)
    for e in range(8):
        columns = turned(rest[e], mid[e])
        for half in range(2):
            for u in (4, 5):
                start = 64 * half + 32 * (u - 4)
                out[u // STEPS, u % STEPS, e + 8 * half] = columns[start : start + 32]


def ordered(back):
    return pl.pallas_call(
        order_kernel,
        grid=(2,),
        in_specs=[vmem()],
        out_specs=pl.BlockSpec((2, STEPS, 16, 32, 96), lambda g: (0, 0, g, 0, 0)),
        out_shape=jax.ShapeDtypeStruct((2, STEPS, 32, 32, 96), jnp.bfloat16),
        compiler_params=limit(24),
        cost_estimate=pl.CostEstimate(flops=0, bytes_accessed=4 << 20, transcendentals=0),
        name="order",
    )(back.reshape(2, 2, 16, ROWS, LANES))


def per_device(signal, valid, owners):
    chunks = placed(whitened(signal, valid)).reshape(128, 2, 48, LANES)
    got = lax.all_to_all(chunks, ("zh", "zl", "core", "x", "y"), 0, 0, tiled=True)
    got = got.reshape(2, 2, 32, 2, 48, LANES)
    own, columns = picked(owners, got)
    other = lax.ppermute(own, "core", [(0, 1), (1, 0)])
    result = cross_mid(got, own, other, cross_full(got, columns))
    back = lax.all_to_all(result, ("zh", "core", "x", "y"), 0, 0, tiled=True)
    return jnp.transpose(ordered(back), (0, 1, 4, 2, 3))


def solution(mesh):
    chan = ("y", "x", "zh", "core")
    fine = Mesh(mesh.devices.reshape(4, 4, 2, 2, 2), chan + ("zl",))
    in_specs = (P(chan, "zl", None), P(chan, "zl"), P())
    out_specs = P(None, None, "zl", chan, None)
    return jax.shard_map(
        per_device, mesh=fine, in_specs=in_specs, out_specs=out_specs, check_vma=False
    )
```

```python
import math

import jax
import jax.numpy as jnp
from jax import lax
from jax.experimental import pallas as pl
from jax.experimental.pallas import tpu as pltpu
from jax.sharding import Mesh
from jax.sharding import PartitionSpec as P

SAMPLES = 1024
BINS = 192
WINDOWS = 256
STEPS = 3
CH_DEV = 32
N_CHAN = 64
LANES = 128
COLUMNS = 2 * STEPS * CH_DEV
FULL_ROWS, ROWS = 48, 72
CHUNKS = ((0, 8), (8, 20), (20, 32))


def vmem():
    return pl.BlockSpec(memory_space=pltpu.VMEM)


def limit(mib):
    return pltpu.CompilerParams(vmem_limit_bytes=mib << 20)


def angles(rows, scale):
    times = lax.broadcasted_iota(jnp.int32, (rows, SAMPLES), 1)
    freqs = lax.broadcasted_iota(jnp.int32, (rows, SAMPLES), 0) * scale
    return (freqs * times % SAMPLES).astype(jnp.float32) * (2.0 * math.pi / SAMPLES)


def fill_table(table):
    fine = angles(32, 1)
    coarse = angles(8, 32)
    times = lax.broadcasted_iota(jnp.int32, (1, SAMPLES), 1).astype(jnp.float32)
    taper = 0.5 - 0.5 * jnp.cos(times * (2.0 * math.pi / SAMPLES))
    fine_cos, fine_sin = jnp.cos(fine) * taper, jnp.sin(fine) * taper
    coarse_cos, coarse_sin = jnp.cos(coarse), jnp.sin(coarse)
    for a in range(6):
        cos_a, sin_a = coarse_cos[a + 1 : a + 2], coarse_sin[a + 1 : a + 2]
        real = cos_a * fine_cos - sin_a * fine_sin
        imag = -sin_a * fine_cos - cos_a * fine_sin
        table[32 * a : 32 * a + 32, :] = real.astype(jnp.bfloat16)
        table[BINS + 32 * a : BINS + 32 * a + 32, :] = imag.astype(jnp.bfloat16)


def whiten_kernel(signal, valid, white, samples, usable, table, sems):
    copies = [pltpu.make_async_copy(valid, usable, sems.at[len(CHUNKS)])]
    for k, (start, end) in enumerate(CHUNKS):
        copies.append(
            pltpu.make_async_copy(signal.at[start:end], samples.at[start:end], sems.at[k])
        )
    for copy in copies[:3]:
        copy.start()
    fill_table(table)
    copies[0].wait()
    weights = usable[...].astype(jnp.float32)
    arrives = {start: copy for (start, _), copy in zip(CHUNKS, copies[1:])}
    for c0 in range(0, CH_DEV, 2):
        if c0 in arrives:
            arrives[c0].wait()
            if c0 == 0:
                copies[3].start()
        both = samples[c0 : c0 + 2].reshape(2 * LANES, SAMPLES)
        spec = lax.dot_general(
            table[...], both, (((1,), (1,)), ((), ())), preferred_element_type=jnp.float32
        )
        power = jnp.sum(spec * spec, axis=0, keepdims=True) * (1.0 / BINS)
        factor = lax.rsqrt(power + 1e-06)
        for one in range(2):
            lanes = slice(one * LANES, (one + 1) * LANES)
            scale = factor[:, lanes] * weights[c0 + one : c0 + one + 1, :]
            white[c0 + one] = (spec[:, lanes] * scale).astype(jnp.bfloat16)


def whitened(signal, valid):
    signal = pltpu.with_memory_space_constraint(signal, pltpu.HBM)
    valid = pltpu.with_memory_space_constraint(valid, pltpu.HBM)
    return pl.pallas_call(
        whiten_kernel,
        in_specs=[pl.BlockSpec(memory_space=pltpu.HBM)] * 2,
        out_specs=vmem(),
        out_shape=jax.ShapeDtypeStruct((CH_DEV, 2 * BINS, LANES), jnp.bfloat16),
        scratch_shapes=[
            pltpu.VMEM((CH_DEV, LANES, SAMPLES), jnp.bfloat16),
            pltpu.VMEM((CH_DEV, LANES), jnp.int32),
            pltpu.VMEM((2 * BINS, SAMPLES), jnp.bfloat16),
            pltpu.SemaphoreType.DMA((len(CHUNKS) + 1,)),
        ],
        compiler_params=limit(40),
        cost_estimate=pl.CostEstimate(
            flops=2 * 2 * BINS * SAMPLES * 4096, bytes_accessed=12 << 20, transcendentals=0
        ),
        name="whiten",
    )(signal, valid)


def place_kernel(white, out):
    for g in range(2):
        c = slice(16 * g, 16 * g + 16)
        for h in range(2):
            for r in range(2):
                for m in range(3):
                    start = BINS * r + 96 * h + 32 * m
                    rows = jnp.swapaxes(white[c, start : start + 32, :], 0, 1)
                    rows = rows.reshape(2, 16, 16, LANES)
                    if m == 2:
                        out[:, h, g, :, r, 32:48, :] = rows
                    else:
                        out[m, h, :, :, r, c, :] = rows


def placed(white):
    return pl.pallas_call(
        place_kernel,
        in_specs=[vmem()],
        out_specs=vmem(),
        out_shape=jax.ShapeDtypeStruct((2, 2, 2, 16, 2, 48, LANES), jnp.bfloat16),
        compiler_params=limit(16),
        cost_estimate=pl.CostEstimate(flops=0, bytes_accessed=6 << 20, transcendentals=0),
        name="place",
    )(white)


def planned_columns(planned):
    real = [jnp.concatenate([b[0, 0], b[0, 1], b[1, 0], b[1, 1]], axis=1) for b in planned]
    imag = [jnp.concatenate([-b[0, 1], b[0, 0], -b[1, 1], b[1, 0]], axis=1) for b in planned]
    return jnp.concatenate(real + imag, axis=0)


def pick_kernel(owners, got, own, columns):
    planned = []
    for s in range(STEPS):
        owner = owners[0, s]
        y, x = lax.shift_right_logical(owner, 4), lax.shift_right_logical(owner, 2) & 3
        zh, core = lax.shift_right_logical(owner, 1) & 1, owner & 1
        at = core * 16 + x * 4 + y
        own[s] = got[zh, :, at, :, 32:48, :]
        planned.append(got[zh, :, at, :, :32, :])
    columns[...] = planned_columns(planned)


def picked(owners, got):
    return pl.pallas_call(
        pick_kernel,
        in_specs=[vmem(), vmem()],
        out_specs=[vmem(), vmem()],
        out_shape=[
            jax.ShapeDtypeStruct((STEPS, 2, 2, 16, LANES), jnp.bfloat16),
            jax.ShapeDtypeStruct((COLUMNS, 4 * LANES), jnp.bfloat16),
        ],
        compiler_params=limit(16),
        cost_estimate=pl.CostEstimate(flops=0, bytes_accessed=98304, transcendentals=0),
        name="pick",
    )(owners.reshape(1, STEPS), got)


def products(left, columns):
    count, channels = left.shape[1], left.shape[3]
    rows = jnp.concatenate(
        [left[w, :, r].reshape(count * channels, LANES) for w in range(2) for r in range(2)], axis=1
    )
    result = lax.dot_general(
        rows, columns, (((1,), (1,)), ((), ())), preferred_element_type=jnp.float32
    )
    return (result * (1.0 / math.sqrt(WINDOWS))).reshape(count, channels, COLUMNS)


def packed(result):
    rest = result[:, :, LANES:]
    parts = [result[:, :, :LANES]]
    for start in range(0, result.shape[1], 16):
        parts.append(
            jnp.concatenate([rest[:, start : start + 8], rest[:, start + 8 : start + 16]], axis=2)
        )
    return jnp.concatenate(parts, axis=1).astype(jnp.bfloat16)


def full_kernel(got, columns, out):
    for start in range(0, N_CHAN, 8):
        zh, at = divmod(start, 32)
        left = got[zh, :, at : at + 8, :, :32, :]
        out[start : start + 8, :FULL_ROWS, :] = packed(products(left, columns[...]))


def cross_full(got, columns):
    return pl.pallas_call(
        full_kernel,
        in_specs=[vmem(), vmem()],
        out_specs=vmem(),
        out_shape=jax.ShapeDtypeStruct((N_CHAN, ROWS, LANES), jnp.bfloat16),
        compiler_params=limit(16),
        cost_estimate=pl.CostEstimate(
            flops=2 * 2048 * 512 * 192, bytes_accessed=3 << 20, transcendentals=0
        ),
        name="cross_full",
    )(got, columns)


def mid_kernel(got, own, other, partial, out, columns):
    del partial
    first = lax.axis_index("core") == 0
    planned = []
    for s in range(STEPS):
        mine, theirs = own[s], other[s]
        low, high = jnp.where(first, mine, theirs), jnp.where(first, theirs, mine)
        planned.append(jnp.concatenate([low, high], axis=2))
    columns[...] = planned_columns(planned)
    for start in range(0, N_CHAN, 16):
        zh, at = divmod(start, 32)
        left = got[zh, :, at : at + 16, :, 32:48, :]
        out[start : start + 16, FULL_ROWS:, :] = packed(products(left, columns[...]))


def cross_mid(got, own, other, partial):
    return pl.pallas_call(
        mid_kernel,
        in_specs=[vmem()] * 4,
        out_specs=vmem(),
        out_shape=jax.ShapeDtypeStruct((N_CHAN, ROWS, LANES), jnp.bfloat16),
        scratch_shapes=[pltpu.VMEM((COLUMNS, 4 * LANES), jnp.bfloat16)],
        input_output_aliases={3: 0},
        compiler_params=limit(16),
        cost_estimate=pl.CostEstimate(
            flops=2 * 1024 * 512 * 192, bytes_accessed=2 << 20, transcendentals=0
        ),
        name="cross_mid",
    )(got, own, other, partial)


def order_kernel(back, out, held, sems):
    copies = []

    def send(real, steps, channels):
        part = (real, steps, channels)
        copies.append(pltpu.make_async_copy(held.at[part], out.at[part], sems.at[len(copies)]))
        copies[-1].start()

    def turned(full, mid):
        return jnp.concatenate([full, mid], axis=0).T

    for g in range(2):
        first, packed_row = 16 * g, 32 + 8 * g
        channels = slice(first, first + 16)
        full = jnp.swapaxes(back[:, :, :, channels, :].reshape(N_CHAN, 16, LANES), 0, 1)
        mid = jnp.swapaxes(back[:, g, :, 48:64, :].reshape(32, 16, LANES), 0, 1)
        for c in range(16):
            columns = turned(full[c], mid[c])
            for u in range(4):
                held[u // STEPS, u % STEPS, first + c] = columns[32 * u : 32 * u + 32]
        send(0, slice(0, STEPS), channels)
        send(1, slice(0, 1), channels)
        rest = back[:, :, :, packed_row : packed_row + 8, :].astype(jnp.float32)
        rest = jnp.swapaxes(rest.reshape(N_CHAN, 8, LANES), 0, 1).astype(jnp.bfloat16)
        mid = back[:, g, :, 64:72, :].astype(jnp.float32).reshape(32, 8, LANES)
        mid = jnp.swapaxes(mid, 0, 1).astype(jnp.bfloat16)
        for e in range(8):
            columns = turned(rest[e], mid[e])
            for half in range(2):
                for u in (4, 5):
                    start = 64 * half + 32 * (u - 4)
                    at = first + e + 8 * half
                    held[u // STEPS, u % STEPS, at] = columns[start : start + 32]
        send(1, slice(1, STEPS), channels)
    for copy in copies:
        copy.wait()


def ordered(back):
    shape = (2, STEPS, 32, 32, 96)
    return pl.pallas_call(
        order_kernel,
        in_specs=[vmem()],
        out_specs=pl.BlockSpec(memory_space=pl.ANY),
        out_shape=jax.ShapeDtypeStruct(shape, jnp.bfloat16),
        scratch_shapes=[pltpu.VMEM(shape, jnp.bfloat16), pltpu.SemaphoreType.DMA((6,))],
        compiler_params=limit(24),
        cost_estimate=pl.CostEstimate(flops=0, bytes_accessed=4 << 20, transcendentals=0),
        name="order",
    )(back.reshape(2, 2, 16, ROWS, LANES))


def per_device(signal, valid, owners):
    chunks = placed(whitened(signal, valid)).reshape(128, 2, 48, LANES)
    got = lax.all_to_all(chunks, ("zh", "zl", "core", "x", "y"), 0, 0, tiled=True)
    got = got.reshape(2, 2, 32, 2, 48, LANES)
    own, columns = picked(owners, got)
    other = lax.ppermute(own, "core", [(0, 1), (1, 0)])
    result = cross_mid(got, own, other, cross_full(got, columns))
    back = lax.all_to_all(result, ("zh", "core", "x", "y"), 0, 0, tiled=True)
    return jnp.transpose(ordered(back), (0, 1, 4, 2, 3))


def solution(mesh):
    chan = ("y", "x", "zh", "core")
    fine = Mesh(mesh.devices.reshape(4, 4, 2, 2, 2), chan + ("zl",))
    in_specs = (P(chan, "zl", None), P(chan, "zl"), P())
    out_specs = P(None, None, "zl", chan, None)
    return jax.shard_map(
        per_device, mesh=fine, in_specs=in_specs, out_specs=out_specs, check_vma=False
    )
```
